256 devices in a mesh: seq: 64 (over x, z, core), head: 4 (over y).
Axes of the slice: x: 4, y: 4, z: 8, core: 2. Of those that a mesh axis runs over, the one named last changes fastest.
Arguments:
- queries: bfloat16 [65536, 2048], P('seq', 'head'), may hold values from -1.796875 to 1.796875
- keys: bfloat16 [65536, 2048], P('seq', 'head'), may hold values from -1.796875 to 1.796875
- values: bfloat16 [65536, 2048], P('seq', 'head'), may hold values from -16 to 16
- grad_out: bfloat16 [65536, 2048], P('seq', 'head'), may hold values from -1.1953125 to 1.1953125
Outputs:
- output: bfloat16 [65536, 2048], P('seq', 'head')
- grad_query: bfloat16 [65536, 2048], P('seq', 'head')
- grad_key: bfloat16 [65536, 2048], P('seq', 'head')
- grad_value: bfloat16 [65536, 2048], P('seq', 'head')
The draws below stay inside these ranges and needn't reach their ends.
All inputs are finite; a program needn't handle non-finite values.
Results may differ from the reference program's by a relative error of at most 0.0065.
Values sent between devices are 32-bit elements; how exact they have to be, the bound alone decides.
A program may use at most 128 MiB of HBM per device.

```python
import jax
import jax.numpy as jnp
from jax import lax

HEADS = 16
HEAD_DIM = 128
TOK_DEV = 1024
TOKENS = 65536


def draw_values(key, part):
    key_scale, key_body = jax.random.split(key, 2)
    head_index = jnp.arange(HEADS, dtype=jnp.float32)
    jitter = jax.random.uniform(key_scale, (HEADS,), jnp.float32)
    head_scale = 0.4 * 10.0 ** ((head_index + jitter) / HEADS)
    base = jnp.clip(jax.random.normal(key_body, (TOKENS, HEADS, HEAD_DIM), jnp.float32), -4.0, 4.0)
    return (base * head_scale[None, :, None]).reshape(TOKENS, HEADS * HEAD_DIM).astype(jnp.bfloat16)


def block_levels(key, dims, cuts, low, high):
    def one(dim, parts):
        draws = jax.random.uniform(jax.random.fold_in(jax.random.fold_in(key, 6), dim), (parts,), jnp.float32, low / len(cuts), high / len(cuts))
        return jnp.repeat(jnp.exp(draws), dims[dim] // parts).reshape((-1,) + (1,) * (len(dims) - dim - 1))

    gain = one(*cuts[0])
    for cut in cuts[1:]:
        gain = gain * one(*cut)
    return gain


def normal_values(rng, shape, width, most, cuts=(), kind=jnp.bfloat16):
    level = block_levels(rng, shape, cuts, -0.22, 0.18) if cuts else 1.0
    result = jax.random.normal(rng, shape, jnp.float32) * width * level
    return jnp.minimum(jnp.maximum(result, -most), most).astype(kind)


def setup_inputs(seed: int = 0) -> dict:
    streams_of = jax.random.split(jax.random.key(seed), 5)
    queries = normal_values(streams_of[0], (TOKENS, HEADS * HEAD_DIM), 0.3, 1.796875, ((0, 64), (1, 4)))
    keys = normal_values(streams_of[1], (TOKENS, HEADS * HEAD_DIM), 0.3, 1.796875, ((0, 64), (1, 4)))
    values = draw_values(jax.random.fold_in(streams_of[4], 71), 0)
    grad_out = normal_values(streams_of[3], (TOKENS, HEADS * HEAD_DIM), 0.2, 1.1953125, ((0, 64), (1, 4)))
    return {"queries": queries, "keys": keys, "values": values, "grad_out": grad_out}


EPSILON = 1e-06

def rounded(tensor):
    return lax.optimization_barrier(tensor.astype(jnp.bfloat16)).astype(jnp.float32)

def causal_scores(query_side, key_side):
    raw_scores = jnp.einsum('thd,shd->hts', query_side, key_side)
    row_index = jnp.arange(query_side.shape[0], dtype=jnp.int32)
    keep = row_index[:, None] >= row_index[None, :]
    return rounded(jnp.where(keep[None], raw_scores, jnp.zeros_like(raw_scores)))

def reference(queries, keys, values, grad_out):
    n_blocks = TOKENS // TOK_DEV
    block_shape = (n_blocks, TOK_DEV, HEADS, HEAD_DIM)
    query_blocks = queries.reshape(block_shape)
    key_blocks = keys.reshape(block_shape)
    value_blocks = values.reshape(block_shape)

    def forward_step(prefix, block_data):
        query_block = block_data[0].astype(jnp.float32)
        key_block = block_data[1].astype(jnp.float32)
        value_block = block_data[2].astype(jnp.float32)
        scores = causal_scores(query_block, key_block)
        mixed = jnp.einsum('hts,she->the', scores, value_block)
        mixed = mixed + jnp.einsum('thd,hde->the', query_block, rounded(prefix))
        local_state = jnp.einsum('thd,the->hde', key_block, value_block)
        return (prefix + local_state, (mixed, prefix))
    zero_state = jnp.zeros((HEADS, HEAD_DIM, HEAD_DIM), jnp.float32)
    unused, (mixed, prefixes) = lax.scan(forward_step, zero_state, (query_blocks, key_blocks, value_blocks))
    mixed_rows = mixed.reshape(TOKENS, HEADS * HEAD_DIM)
    inverse_rms = lax.rsqrt(lax.optimization_barrier(jnp.mean(mixed_rows * mixed_rows, axis=1, keepdims=True)) + EPSILON)
    normed = mixed_rows * inverse_rms
    output = normed.astype(jnp.bfloat16)
    grad_float = grad_out.astype(jnp.float32)
    cross_mean = lax.optimization_barrier(jnp.mean(grad_float * normed, axis=1, keepdims=True))
    grad_mixed = (inverse_rms * (grad_float - normed * cross_mean)).astype(jnp.bfloat16)
    grad_blocks = grad_mixed.reshape(block_shape)

    def grad_state(block_data):
        return jnp.einsum('thd,the->hde', block_data[0].astype(jnp.float32), block_data[1].astype(jnp.float32))
    local_grads = lax.map(grad_state, (query_blocks, grad_blocks))

    def suffix_step(carry, term):
        return (carry + term, carry)
    unused_two, suffixes = lax.scan(suffix_step, zero_state, local_grads, reverse=True)

    def backward_block(block_data):
        query_block = block_data[0].astype(jnp.float32)
        key_block = block_data[1].astype(jnp.float32)
        value_block = block_data[2].astype(jnp.float32)
        grad_block = block_data[3].astype(jnp.float32)
        prefix_round = rounded(block_data[4])
        suffix_round = rounded(block_data[5])
        scores = causal_scores(query_block, key_block)
        grad_scores = causal_scores(grad_block, value_block)
        grad_q = jnp.einsum('hts,shd->thd', grad_scores, key_block) + jnp.einsum('the,hde->thd', grad_block, prefix_round)
        grad_k = jnp.einsum('hts,thd->shd', grad_scores, query_block) + jnp.einsum('she,hde->shd', value_block, suffix_round)
        grad_v = jnp.einsum('hts,the->she', scores, grad_block) + jnp.einsum('shd,hde->she', key_block, suffix_round)
        return (grad_q.astype(jnp.bfloat16), grad_k.astype(jnp.bfloat16), grad_v.astype(jnp.bfloat16))
    grad_q, grad_k, grad_v = lax.map(backward_block, (query_blocks, key_blocks, value_blocks, grad_blocks, prefixes, suffixes))
    flat_shape = (TOKENS, HEADS * HEAD_DIM)
    return (output, grad_q.reshape(flat_shape), grad_k.reshape(flat_shape), grad_v.reshape(flat_shape))
```

```python
import functools

import jax
import jax.numpy as jnp
from jax import lax
from jax.experimental import pallas as pl
from jax.experimental.pallas import tpu as pltpu
from jax.sharding import PartitionSpec as P

HEADS = 16
HEAD_DIM = 128
EPSILON = 1e-06
CHIPS_X = 4
CHUNK = 256
MESH = pl.DeviceIdType.MESH
F32 = jnp.float32
BF16 = jnp.bfloat16


def nn(a, b):
    return lax.dot_general(a, b, (((1,), (0,)), ((), ())), preferred_element_type=F32)


def nt(a, b):
    return lax.dot_general(a, b, (((1,), (1,)), ((), ())), preferred_element_type=F32)


def tn(a, b):
    return lax.dot_general(a, b, (((0,), (0,)), ((), ())), preferred_element_type=F32)


def split2(v):
    hi = v.astype(BF16)
    return hi, (v - hi.astype(F32)).astype(BF16)


def kernel(
    chips_z, n_head,
    q_hbm, k_hbm, v_hbm, g_hbm,
    o_hbm, gq_hbm, gk_hbm, gv_hbm,
    q, k, v, g, qt, mixed, gm, score_t, gk_part, gv_part, o_v, gq_v, gk_v, gv_v,
    cum, gs_part, st, cx, ps, rb, ds, rd, cs, full, diag, ysend, yrecv,
    load_sem, out_sem, core_send, core_recv, b_send, b_recv, d_send, d_recv, y_send_sem, y_recv_sem,
):
    tokens, width = q.shape
    n_local = width // HEAD_DIM
    n_pair = n_local // 2
    half_rows = n_pair * HEAD_DIM
    n_chunk = tokens // CHUNK
    n_chip = CHIPS_X * chips_z
    full_width = n_local * n_head * HEAD_DIM

    seq = lax.axis_index("seq")
    row = lax.axis_index("head")
    core = lax.rem(seq, 2)
    other = 1 - core
    chip = seq // 2
    x = chip // chips_z
    z = lax.rem(chip, chips_z)

    def far(n, d):
        return min(d, n - d)

    offsets = [(dx, dz) for dx in range(CHIPS_X) for dz in range(chips_z) if dx or dz]
    offsets.sort(key=lambda o: (-far(chips_z, o[1]), -far(CHIPS_X, o[0])))
    peers = [lax.rem(x + dx, CHIPS_X) * chips_z + lax.rem(z + dz, chips_z) for dx, dz in offsets]
    rows_of = [lax.rem(row + d, n_head) for d in range(1, n_head)]

    barrier = pltpu.get_barrier_semaphore()
    for p in peers:
        pl.semaphore_signal(barrier, inc=1, device_id=(p * 2 + core, row), device_id_type=MESH)
    for r in rows_of:
        pl.semaphore_signal(barrier, inc=1, device_id=(seq, r), device_id_type=MESH)
    pl.semaphore_signal(barrier, inc=1, device_id=(chip * 2 + other, row), device_id_type=MESH)

    loads = [
        pltpu.make_async_copy(src, dst, load_sem.at[i])
        for i, (src, dst) in enumerate(((k_hbm, k), (v_hbm, v), (q_hbm, q), (g_hbm, g)))
    ]
    for copy in loads:
        copy.start()

    def rows(j):
        return pl.ds(j * CHUNK, CHUNK) if isinstance(j, int) else pl.ds(pl.multiple_of(j * CHUNK, CHUNK), CHUNK)

    def cols(h):
        return pl.ds(h * HEAD_DIM, HEAD_DIM)

    def pair_cols(p):
        return pl.ds(p * 2 * HEAD_DIM, 2 * HEAD_DIM)

    own_rows = pl.ds(pl.multiple_of(core * half_rows, half_rows), half_rows)
    other_rows = pl.ds(pl.multiple_of(other * half_rows, half_rows), half_rows)

    row_id = lax.broadcasted_iota(jnp.int32, (CHUNK, CHUNK), 0)
    col_id = lax.broadcasted_iota(jnp.int32, (CHUNK, CHUNK), 1)

    def lower(s):
        return jnp.where(row_id >= col_id, s, 0.0).astype(BF16)

    def upper(s):
        return jnp.where(row_id <= col_id, s, 0.0).astype(BF16)

    def core_copy(s, stage):
        if stage == 0:
            src, dst = st.at[s, other_rows], cx.at[s]
        else:
            src, dst = cs.at[s], full.at[s, own_rows]
        return pltpu.make_async_remote_copy(
            src_ref=src, dst_ref=dst, send_sem=core_send.at[s, stage], recv_sem=core_recv.at[s, stage],
            device_id=(chip * 2 + other, row), device_id_type=MESH,
        )

    def to_owners(s):
        core_copy(s, 0).wait_recv()
        ps[s] = (st[s, own_rows, :] + cx[s]).reshape(ps.shape[1:])
        for p in peers:
            pltpu.make_async_remote_copy(
                src_ref=ps.at[s, p], dst_ref=rb.at[s, chip], send_sem=b_send.at[s], recv_sem=b_recv.at[s],
                device_id=(p * 2 + core, row), device_id_type=MESH,
            ).start()
        rb[s, chip] = ps[s, chip]

    def wait_all(ref, s, sem):
        part = ref.at[s, pl.ds(0, n_chip - 1)]
        pltpu.make_async_copy(part, part, sem.at[s]).wait()

    def from_owners(s):
        wait_all(rb, s, b_recv)
        total = jnp.zeros(rb.shape[2:], F32)
        for i in range(n_chip) if s == 0 else range(n_chip - 1, -1, -1):
            ds[s, i] = total
            total = total + rb[s, i]
        for p in peers:
            pltpu.make_async_remote_copy(
                src_ref=ds.at[s, p], dst_ref=rd.at[s, chip], send_sem=d_send.at[s], recv_sem=d_recv.at[s],
                device_id=(p * 2 + core, row), device_id_type=MESH,
            ).start()
        rd[s, chip] = ds[s, chip]

    def between_cores(s):
        wait_all(rd, s, d_recv)
        half = rd[s].reshape(half_rows, HEAD_DIM)
        first = core == s
        cs[s] = jnp.where(first, half + st[s, own_rows, :], half)
        full[s, own_rows, :] = jnp.where(first, half, half + cx[s])
        core_copy(s, 1).start()

    def fill_diag(s):
        for p in range(n_pair):
            for i in range(2):
                block = full[s, pl.ds((2 * p + i) * HEAD_DIM, HEAD_DIM), :].astype(BF16)
                diag[s, p, pl.ds(i * HEAD_DIM, HEAD_DIM), pl.ds(i * HEAD_DIM, HEAD_DIM)] = block

    diag[...] = jnp.zeros_like(diag)

    loads[0].wait()
    loads[1].wait()
    for h in range(n_local):
        total = None
        for j in range(n_chunk):
            if j:
                cum[j, pl.ds(h * HEAD_DIM, HEAD_DIM), :] = total
            new = tn(k[rows(j), cols(h)], v[rows(j), cols(h)])
            total = new if total is None else total + new
        cum[0, pl.ds(h * HEAD_DIM, HEAD_DIM), :] = jnp.zeros_like(total)
        st[0, pl.ds(h * HEAD_DIM, HEAD_DIM), :] = total

    pl.semaphore_wait(barrier, len(peers) + len(rows_of) + 1)
    core_copy(0, 0).start()
    loads[2].wait()
    for h in range(n_local):
        for j in range(n_chunk):
            qt[pl.ds(h * HEAD_DIM, HEAD_DIM), rows(j)] = q[rows(j), cols(h)].T
    to_owners(0)

    @pl.loop(0, n_chunk)
    def _(j):
        for h in range(n_local):
            q_c, k_c, v_c = q[rows(j), cols(h)], k[rows(j), cols(h)], v[rows(j), cols(h)]
            before = cum[j, pl.ds(h * HEAD_DIM, HEAD_DIM), :].astype(BF16)
            mixed[rows(j), cols(h)] = nn(lower(nt(q_c, k_c)), v_c) + nn(q_c, before)

    from_owners(0)

    @pl.loop(0, n_chunk)
    def _(j):
        for h in range(n_local):
            score_t[j, h] = upper(nt(k[rows(j), cols(h)], q[rows(j), cols(h)]))

    loads[3].wait()
    between_cores(0)
    core_copy(0, 1).wait_recv()
    fill_diag(0)

    sums = jnp.zeros((2 * n_chunk, CHUNK), F32)
    pick = lax.broadcasted_iota(jnp.int32, (2 * n_chunk, HEAD_DIM), 0)
    for j in range(n_chunk):
        squares = jnp.zeros((CHUNK, HEAD_DIM), F32)
        cross = jnp.zeros((CHUNK, HEAD_DIM), F32)
        for p in range(n_pair):
            m = mixed[rows(j), pair_cols(p)] + nn(q[rows(j), pair_cols(p)], diag[0, p])
            mixed[rows(j), pair_cols(p)] = m
            s2 = m * m
            sg = m * g[rows(j), pair_cols(p)].astype(F32)
            squares += s2[:, :HEAD_DIM] + s2[:, HEAD_DIM:]
            cross += sg[:, :HEAD_DIM] + sg[:, HEAD_DIM:]
        for value, at in ((squares, j), (cross, n_chunk + j)):
            one = jnp.where(pick == at, 1.0, 0.0).astype(BF16)
            for piece in split2(value):
                sums += nt(one, piece)
    ysend[...] = sums
    ycopies = [
        pltpu.make_async_remote_copy(
            src_ref=ysend, dst_ref=yrecv.at[row], send_sem=y_send_sem.at[i], recv_sem=y_recv_sem,
            device_id=(seq, r), device_id_type=MESH,
        )
        for i, r in enumerate(rows_of)
    ]
    for copy in ycopies:
        copy.start()
    yrecv[row] = sums
    part = yrecv.at[pl.ds(0, n_head - 1)]
    pltpu.make_async_copy(part, part, y_recv_sem).wait()
    sums = yrecv[0]
    for i in range(1, n_head):
        sums = sums + yrecv[i]
    mean = sums * (1.0 / full_width)
    inverse = lax.rsqrt(mean[:n_chunk] + EPSILON)
    slope = inverse * inverse * mean[n_chunk:]
    per_token = jnp.concatenate([inverse, slope], axis=0).T

    for j in range(n_chunk):
        inv_c = per_token[:, j : j + 1]
        slope_c = per_token[:, n_chunk + j : n_chunk + j + 1]
        for h in range(n_local):
            m = mixed[rows(j), cols(h)]
            gm_c = (inv_c * (g[rows(j), cols(h)].astype(F32) - m * slope_c)).astype(BF16)
            gm[rows(j), cols(h)] = gm_c
            o_v[rows(j), cols(h)] = (m * inv_c).astype(BF16)
            at = pl.ds(h * HEAD_DIM, HEAD_DIM)
            new = nn(qt[at, rows(j)], gm_c)
            gs_part[j, at, :] = new
            st[1, at, :] = new if j == 0 else st[1, at, :] + new
    core_copy(1, 0).start()
    out_o = pltpu.make_async_copy(o_v, o_hbm, out_sem.at[0])
    out_o.start()
    to_owners(1)

    @pl.loop(0, n_chunk)
    def _(j):
        for h in range(n_local):
            at = pl.ds(h * HEAD_DIM, HEAD_DIM)
            gm_c = gm[rows(j), cols(h)]
            before = (full[0, at, :] + cum[j, at, :]).astype(BF16)
            score = lower(nt(gm_c, v[rows(j), cols(h)]))
            gq_v[rows(j), cols(h)] = (nn(score, k[rows(j), cols(h)]) + nt(gm_c, before)).astype(BF16)

    from_owners(1)
    out_q = pltpu.make_async_copy(gq_v, gq_hbm, out_sem.at[1])
    out_q.start()

    for h in range(n_local):
        at = pl.ds(h * HEAD_DIM, HEAD_DIM)
        after = jnp.zeros((HEAD_DIM, HEAD_DIM), F32)
        for j in range(n_chunk - 1, -1, -1):
            new = gs_part[j, at, :]
            gs_part[j, at, :] = after
            after = after + new

    @pl.loop(0, n_chunk)
    def _(j):
        for h in range(n_local):
            at = pl.ds(h * HEAD_DIM, HEAD_DIM)
            gm_c, v_c, k_c = gm[rows(j), cols(h)], v[rows(j), cols(h)], k[rows(j), cols(h)]
            after = gs_part[j, at, :].astype(BF16)
            score = upper(nt(v_c, gm_c))
            gk_part[rows(j), cols(h)] = nn(score, q[rows(j), cols(h)]) + nt(v_c, after)
            gv_part[rows(j), cols(h)] = nn(score_t[j, h], gm_c) + nn(k_c, after)

    between_cores(1)
    core_copy(1, 1).wait_recv()
    fill_diag(1)
    for p in range(n_pair):
        for j in range(n_chunk):
            gk = gk_part[rows(j), pair_cols(p)] + nt(v[rows(j), pair_cols(p)], diag[1, p])
            gk_v[rows(j), pair_cols(p)] = gk.astype(BF16)
            gv = gv_part[rows(j), pair_cols(p)] + nn(k[rows(j), pair_cols(p)], diag[1, p])
            gv_v[rows(j), pair_cols(p)] = gv.astype(BF16)
    out_k = pltpu.make_async_copy(gk_v, gk_hbm, out_sem.at[2])
    out_v = pltpu.make_async_copy(gv_v, gv_hbm, out_sem.at[3])
    out_k.start()
    out_v.start()
    for copy in ycopies:
        copy.wait_send()
    for s in range(2):
        for stage in range(2):
            core_copy(s, stage).wait_send()
        wait_all(ps, s, b_send)
        wait_all(ds, s, d_send)
    for copy in (out_o, out_q, out_k, out_v):
        copy.wait()


def solution(mesh):
    chips_z = mesh.shape["seq"] // (2 * CHIPS_X)
    n_head = mesh.shape["head"]

    def shards(queries, keys, values, grad_out):
        tokens, width = queries.shape
        n_local = width // HEAD_DIM
        n_chunk = tokens // CHUNK
        n_chip = CHIPS_X * chips_z
        half = width // 2
        piece = half // n_chip
        wide = lambda dtype: pltpu.VMEM((tokens, width), dtype)
        scratch = [
            wide(BF16), wide(BF16), wide(BF16), wide(BF16),
            pltpu.VMEM((width, tokens), BF16),
            wide(F32),
            wide(BF16),
            pltpu.VMEM((n_chunk, n_local, CHUNK, CHUNK), BF16),
            wide(F32), wide(F32),
            wide(BF16), wide(BF16), wide(BF16), wide(BF16),
            pltpu.VMEM((n_chunk, width, HEAD_DIM), F32),
            pltpu.VMEM((n_chunk, width, HEAD_DIM), F32),
            pltpu.VMEM((2, width, HEAD_DIM), F32),
            pltpu.VMEM((2, half, HEAD_DIM), F32),
            pltpu.VMEM((2, n_chip, piece, HEAD_DIM), F32),
            pltpu.VMEM((2, n_chip, piece, HEAD_DIM), F32),
            pltpu.VMEM((2, n_chip, piece, HEAD_DIM), F32),
            pltpu.VMEM((2, n_chip, piece, HEAD_DIM), F32),
            pltpu.VMEM((2, half, HEAD_DIM), F32),
            pltpu.VMEM((2, width, HEAD_DIM), F32),
            pltpu.VMEM((2, n_local // 2, 2 * HEAD_DIM, 2 * HEAD_DIM), BF16),
            pltpu.VMEM((2 * n_chunk, CHUNK), F32),
            pltpu.VMEM((n_head, 2 * n_chunk, CHUNK), F32),
            pltpu.SemaphoreType.DMA((4,)),
            pltpu.SemaphoreType.DMA((4,)),
            pltpu.SemaphoreType.DMA((2, 2)),
            pltpu.SemaphoreType.DMA((2, 2)),
            pltpu.SemaphoreType.DMA((2,)),
            pltpu.SemaphoreType.DMA((2,)),
            pltpu.SemaphoreType.DMA((2,)),
            pltpu.SemaphoreType.DMA((2,)),
            pltpu.SemaphoreType.DMA((n_head - 1,)),
            pltpu.SemaphoreType.DMA,
        ]
        return pl.pallas_call(
            functools.partial(kernel, chips_z, n_head),
            out_shape=[jax.ShapeDtypeStruct((tokens, width), BF16)] * 4,
            in_specs=[pl.BlockSpec(memory_space=pl.ANY)] * 4,
            out_specs=[pl.BlockSpec(memory_space=pl.ANY)] * 4,
            scratch_shapes=scratch,
            compiler_params=pltpu.CompilerParams(
                collective_id=0, has_side_effects=True, vmem_limit_bytes=48 * 1024 * 1024
            ),
            cost_estimate=pl.CostEstimate(flops=4_000_000_000, bytes_accessed=8 << 20, transcendentals=4096),
        )(queries, keys, values, grad_out)

    spec = P("seq", "head")
    return jax.shard_map(
        shards, mesh=mesh, in_specs=(spec,) * 4, out_specs=(spec,) * 4, check_vma=False
    )
```
